512 devices in a mesh: front: 16 (over y, z_lo), blk: 32 (over z_hi, x, core).
Axes of the slice: x: 4, y: 4, z: 16 (z_hi: 4, z_lo: 4; z = z_hi * 4 + z_lo), core: 2. Of those that a mesh axis runs over, the one named last changes fastest.
Arguments:
- parent_inverse: bfloat16 [16, 4096, 8192], P('front', 'blk'), may hold values from -6 to 6
- child_factor: bfloat16 [16, 5120, 512], P('front', 'blk'), may hold values from -0.078125 to 0.078125
- child_diagonal: float32 [16, 512, 512], P('front', 'blk'), may hold values from -6 to 6
- structure: int32 [16, 40], replicated, may hold values from 0 to 63, as said below
Outputs:
- off_diagonal: float32 [16, 4096, 2, 512], P('front', 'blk')
- child_inverse: float32 [16, 512, 512], P('front', 'blk')
The draws below stay inside these ranges and needn't reach their ends.
Inputs may be any that keep to these rules, and one draw needn't show every extreme that they name: `structure`: each row lists 40 distinct parent block indices in increasing order, and every list contains the last block 63.
All inputs are finite; a program needn't handle non-finite values.
Results may differ from the reference program's by a relative error of at most 0.002.
Values may be sent and summed in bfloat16 or wider, within the bound.
No kernel may reach another device: no remote copies, remote signals or barrier semaphores. Data moves between devices by JAX's collectives and lax.ppermute only.
A program may use at most 64 MiB of HBM per device.

```python
import jax
import jax.numpy as jnp

BS = 128
NPB = 64
NS = 40
NC = 512
NE = 8192
SROWS = 5120
N_FRONT = 16


def draw_structure(key, part):
    key = jax.random.fold_in(key, 7)
    subkeys = jax.random.split(key, N_FRONT)

    def single(subkey):
        chosen = jax.random.permutation(subkey, NPB - 1)[:NS - 1].astype(jnp.int32)
        last_block = jnp.full((1,), NPB - 1, jnp.int32)
        return jnp.sort(jnp.concatenate([chosen, last_block]))
    return jax.vmap(single)(subkeys).astype(jnp.int32)


def level_of(key, dims, pieces, least, largest):
    def one(axis_at, blocks):
        draws = jax.random.uniform(jax.random.fold_in(jax.random.fold_in(key, 6), axis_at), (blocks,), jnp.float32, least / len(pieces), largest / len(pieces))
        return jnp.repeat(jnp.exp(draws), dims[axis_at] // blocks).reshape((-1,) + (1,) * (len(dims) - axis_at - 1))

    level = one(*pieces[0])
    for cut in pieces[1:]:
        level = level * one(*cut)
    return level


def noise(rng, shape, scale, most, cuts=(), dtype=jnp.bfloat16):
    values = scale * jax.random.normal(rng, shape, jnp.float32)
    if cuts:
        values = values * level_of(rng, shape, cuts, -0.22, 0.18)
    return jnp.clip(values, -most, most).astype(dtype)


def setup_inputs(seed: int = 0) -> dict:
    key_list = jax.random.split(jax.random.key(seed), 5)
    parent_inverse = noise(key_list[0], (N_FRONT, NE // 2, NE), 1.0, 6.0, ((0, 16), (1, 32)))
    child_factor = noise(key_list[1], (N_FRONT, SROWS, NC), SROWS ** -0.5, 0.078125, ((0, 16), (1, 32)))
    child_diagonal = noise(key_list[2], (N_FRONT, NC, NC), 1.0, 6.0, ((0, 16), (1, 32)), jnp.float32)
    structure = draw_structure(jax.random.fold_in(key_list[4], 71), 0)
    return dict(parent_inverse=parent_inverse, child_factor=child_factor, child_diagonal=child_diagonal, structure=structure)


def child_terms(parent, factor, diagonal, listing):
    blocks = parent.reshape(NPB, BS, NPB, BS)
    restricted = jnp.take(jnp.take(blocks, listing, axis=0), listing, axis=2)
    restricted = restricted.reshape(NS * BS, NS * BS)
    product = jnp.dot(restricted, factor, preferred_element_type=jnp.float32)
    product_b = product.astype(jnp.bfloat16)
    inverse = diagonal + jnp.dot(factor.T, product_b, preferred_element_type=jnp.float32)
    placed = jnp.zeros((NPB, BS, NC), jnp.float32).at[listing].set(-product.reshape(NS, BS, NC))
    return placed.reshape(NPB * BS, NC), inverse


def reference(parent_inverse, child_factor, child_diagonal, structure):
    placed_all = []
    inverse_all = []
    for front_index in range(N_FRONT):
        base = front_index - front_index % 2
        parent = jnp.concatenate([parent_inverse[base], parent_inverse[base + 1]], axis=0)
        placed, inverse = child_terms(parent, child_factor[front_index], child_diagonal[front_index], structure[front_index])
        placed_all.append(placed)
        inverse_all.append(inverse)
    half_rows = NE // 2
    outputs = []
    for front_index in range(N_FRONT):
        half = front_index % 2
        first = placed_all[front_index][half * half_rows:(half + 1) * half_rows]
        second = placed_all[front_index ^ 1][half * half_rows:(half + 1) * half_rows]
        outputs.append(jnp.stack([first, second], axis=1))
    return jnp.stack(outputs), jnp.stack(inverse_all)
```

```python
import jax
import jax.numpy as jnp
from jax import lax
from jax.experimental import pallas as pl
from jax.experimental.pallas import tpu as pltpu
from jax.sharding import PartitionSpec as P

BS = 128
NPB = 64
NS = 40
NC = 512
SROWS = NS * BS
NZ = 4
NX = 4
NBLK = NZ * NX * 2
ROWS = SROWS // NBLK
NEAR = NX * 2
VMEM = 48 * 1024 * 1024


def ring(value, dz, dx, swap, mirrored=False):
    pairs = []
    for z in range(NZ):
        for x in range(NX):
            for c in range(2):
                s = -1 if mirrored and c else 1
                to = ((z + s * dz) % NZ * NX + (x + s * dx) % NX) * 2 + (c ^ swap)
                pairs.append(((z * NX + x) * 2 + c, to))
    return lax.ppermute(value, "blk", pairs)


def partner(value):
    pairs = [(source, source ^ 1) for source in range(lax.axis_size("front"))]
    return lax.ppermute(value, "front", pairs)


def pick_kernel(listing, rows, out):
    for i in range(NS):
        column = pl.multiple_of(listing[i] * BS, BS)
        out[:, i * BS : (i + 1) * BS] = rows[:, pl.ds(column, BS)]


def pick(listing, rows):
    return pl.pallas_call(
        pick_kernel,
        out_shape=jax.ShapeDtypeStruct((BS, SROWS), jnp.bfloat16),
        in_specs=[
            pl.BlockSpec(memory_space=pltpu.SMEM),
            pl.BlockSpec(memory_space=pltpu.VMEM),
        ],
        out_specs=pl.BlockSpec(memory_space=pltpu.VMEM),
        compiler_params=pltpu.CompilerParams(vmem_limit_bytes=VMEM),
        name="pick",
    )(listing, rows)


GROUPS = ((0,), (-1, 1), (2,))
PIECES = (0, -1, 1, 2)


def product_kernel(info, listing, rows, other_rows, *refs):
    parts = refs[: 2 * len(GROUPS)]
    own_out, other_out, turned, chosen, factor, wide, sems = refs[2 * len(GROUPS) :]
    zh, x, core = info[0], info[1], info[2]
    copies = []
    for swap in range(2):
        for g, offsets in enumerate(GROUPS):
            part = parts[swap * len(GROUPS) + g]
            side = core if swap == 0 else 1 - core
            for p, dx in enumerate(PIECES):
                for n, dz in enumerate(offsets):
                    base = ((zh + dz + NZ) % NZ * NX + (x + dx + NX) % NX) * 2 + side
                    start = pl.multiple_of(base * ROWS, 32)
                    copy = pltpu.make_async_copy(
                        part.at[pl.ds((p * len(offsets) + n) * ROWS, ROWS), :],
                        factor.at[pl.ds(start, ROWS), :],
                        sems.at[len(copies)],
                    )
                    copy.start()
                    copies.append(copy)
    for i in range(NS):
        column = pl.multiple_of(listing[i] * BS, BS)
        wide[0:BS, i * BS : (i + 1) * BS] = rows[:, pl.ds(column, BS)]
    wide[BS:, :] = other_rows[...]
    for copy in copies:
        copy.wait()
    product = jnp.dot(wide[...], factor[...], preferred_element_type=jnp.float32)
    own = jnp.where(info[3] > 0, product[:BS], 0.0)
    other = jnp.where(info[4] > 0, product[BS:], 0.0)
    own_out[...] = -own
    other_out[...] = -other
    turned[:, :BS] = own.T.astype(jnp.bfloat16)
    turned[:, BS:] = other.T.astype(jnp.bfloat16)
    for i in range(2 * NEAR):
        start = pl.multiple_of(info[8 + i] * BS, BS)
        chosen[i * BS : (i + 1) * BS, :] = factor[pl.ds(start, BS), :]


def product(info, listing, rows, other_rows, parts):
    smem = pl.BlockSpec(memory_space=pltpu.SMEM)
    vmem = pl.BlockSpec(memory_space=pltpu.VMEM)
    return pl.pallas_call(
        product_kernel,
        out_shape=[
            jax.ShapeDtypeStruct((BS, NC), jnp.float32),
            jax.ShapeDtypeStruct((BS, NC), jnp.float32),
            jax.ShapeDtypeStruct((NC, 2 * BS), jnp.bfloat16),
            jax.ShapeDtypeStruct((2 * NEAR * BS, NC), jnp.bfloat16),
        ],
        in_specs=[smem, smem, vmem, vmem]
        + [pl.BlockSpec(memory_space=pl.ANY)] * len(parts),
        out_specs=[vmem] * 4,
        scratch_shapes=[
            pltpu.VMEM((SROWS, NC), jnp.bfloat16),
            pltpu.VMEM((2 * BS, SROWS), jnp.bfloat16),
            pltpu.SemaphoreType.DMA((NBLK,)),
        ],
        compiler_params=pltpu.CompilerParams(vmem_limit_bytes=VMEM),
        name="product",
    )(info, listing, rows, other_rows, *parts)


def partial_kernel(turned, chosen, out):
    width = NC // NEAR
    left = jnp.concatenate(
        [turned[s * width : (s + 1) * width, :] for s in range(NEAR)], axis=1
    )
    total = jnp.dot(left, chosen[...], preferred_element_type=jnp.float32)
    tall = total.T
    for d in range(NBLK):
        first = tall[d * 16 : d * 16 + 8]
        second = tall[d * 16 + 8 : d * 16 + 16]
        out[d * 8 : (d + 1) * 8, :] = jnp.concatenate([first, second], axis=1)


def partial(turned, chosen):
    vmem = pl.BlockSpec(memory_space=pltpu.VMEM)
    return pl.pallas_call(
        partial_kernel,
        out_shape=jax.ShapeDtypeStruct((NBLK * 8, BS), jnp.float32),
        in_specs=[vmem, vmem],
        out_specs=vmem,
        compiler_params=pltpu.CompilerParams(vmem_limit_bytes=VMEM),
        name="partial",
    )(turned, chosen)


def total_kernel(terms, diagonal, out):
    half = BS // 2
    for j in range(NEAR):
        tile = terms[j * 8 : (j + 1) * 8, :]
        for z in range(1, NZ):
            at = (z * NEAR + j) * 8
            tile = tile + terms[at : at + 8, :]
        columns = slice(j * half, (j + 1) * half)
        out[0:8, columns] = diagonal[0:8, columns] + tile[:, :half]
        out[8:16, columns] = diagonal[8:16, columns] + tile[:, half:]


def total(terms, diagonal):
    vmem = pl.BlockSpec(memory_space=pltpu.VMEM)
    return pl.pallas_call(
        total_kernel,
        out_shape=jax.ShapeDtypeStruct((NC // NBLK, NC), jnp.float32),
        in_specs=[vmem, vmem],
        out_specs=vmem,
        name="total",
    )(terms, diagonal)


def around_x(value, core):
    right = ring(value, 0, 1, 0)
    left = ring(value, 0, -1, 0)
    far = ring(jnp.where(core == 0, right, left), 0, 1, 0, mirrored=True)
    pieces = jnp.concatenate([value, right, left, far], axis=0)
    return pieces, ring(pieces, 0, 0, 1)


def body(parent_inverse, child_factor, child_diagonal, structure):
    blk = lax.axis_index("blk")
    front = lax.axis_index("front")
    half = front % 2
    zh, x, core = blk // NEAR, blk // 2 % NX, blk % 2
    lists = lax.dynamic_slice_in_dim(structure, front - half, 2, 0)
    listing = lax.dynamic_index_in_dim(lists, half, 0, keepdims=False)
    other_listing = lax.dynamic_index_in_dim(lists, 1 - half, 0, keepdims=False)
    rows = parent_inverse[0]
    mine = child_factor[0]

    up = ring(mine, 1, 0, 0)
    down = ring(mine, -1, 0, 0)
    other_rows = partner(pick(other_listing, rows))
    across = ring(jnp.where(core == 0, up, down), 1, 0, 0, mirrored=True)
    near, near_swapped = around_x(mine, core)
    sides, sides_swapped = around_x(jnp.concatenate([up, down], axis=0), core)
    far, far_swapped = around_x(across, core)

    near_at = zh * NEAR + jnp.arange(NEAR)
    blocks = jnp.stack(
        [half * (NPB // 2) + near_at, (1 - half) * (NPB // 2) + near_at], axis=1
    ).reshape(-1)
    position = jnp.sum((listing[None, :] < blocks[:, None]).astype(jnp.int32), axis=1)
    position = jnp.minimum(position, NS - 1)
    wanted = jnp.stack([half * (NPB // 2) + blk, (1 - half) * (NPB // 2) + blk])
    member = jnp.any(listing[None, :] == wanted[:, None], axis=1).astype(jnp.int32)
    info = jnp.concatenate(
        [jnp.stack([zh, x, core]), member, jnp.zeros((3,), jnp.int32), position]
    )
    own_out, other_out, turned, chosen = product(
        info,
        listing,
        rows,
        other_rows,
        (near, sides, far, near_swapped, sides_swapped, far_swapped),
    )
    second = partner(other_out)
    groups = [[z * NEAR + i for i in range(NEAR)] for z in range(NZ)]
    turned = lax.all_to_all(
        turned, "blk", 0, 0, axis_index_groups=groups, tiled=True
    )
    terms = lax.all_to_all(partial(turned, chosen), "blk", 0, 0, tiled=True)
    inverse = total(terms, child_diagonal[0])
    placed = jnp.stack([own_out, second], axis=1)
    return placed[None], inverse[None]


def solution(mesh):
    in_specs = (P("front", "blk", None), P("front", "blk", None), P("front", "blk", None), P())
    out_specs = (P("front", "blk", None, None), P("front", "blk", None))
    return jax.shard_map(body, mesh=mesh, in_specs=in_specs, out_specs=out_specs, check_vma=False)
```

```python
import jax
import jax.numpy as jnp
from jax import lax
from jax.experimental import pallas as pl
from jax.experimental.pallas import tpu as pltpu
from jax.sharding import PartitionSpec as P

BS = 128
NPB = 64
NS = 40
NC = 512
SROWS = NS * BS
NZ = 4
NX = 4
NBLK = NZ * NX * 2
ROWS = SROWS // NBLK
NEAR = NX * 2
VMEM = 32 * 1024 * 1024


def ring(value, dz, dx, swap, mirrored=False):
    pairs = []
    for z in range(NZ):
        for x in range(NX):
            for c in range(2):
                s = -1 if mirrored and c else 1
                to = ((z + s * dz) % NZ * NX + (x + s * dx) % NX) * 2 + (c ^ swap)
                pairs.append(((z * NX + x) * 2 + c, to))
    return lax.ppermute(value, "blk", pairs)


def partner(value):
    pairs = [(source, source ^ 1) for source in range(lax.axis_size("front"))]
    return lax.ppermute(value, "front", pairs)


SENT = (40,)


def pick_kernel(lists, rows, own, *others):
    for i in range(NS):
        columns = pl.ds(pl.multiple_of(lists[0, i] * BS, BS), BS)
        own[:, i * BS : (i + 1) * BS] = rows[:, columns]
    i = 0
    for n, count in enumerate(SENT):
        for at in range(count):
            columns = pl.ds(pl.multiple_of(lists[1, i] * BS, BS), BS)
            others[n][:, at * BS : (at + 1) * BS] = rows[:, columns]
            i += 1


def pick(lists, rows):
    vmem = pl.BlockSpec(memory_space=pltpu.VMEM)
    return pl.pallas_call(
        pick_kernel,
        out_shape=[pltpu.VMEM((BS, SROWS), jnp.bfloat16)]
        + [jax.ShapeDtypeStruct((BS, count * BS), jnp.bfloat16) for count in SENT],
        in_specs=[pl.BlockSpec(memory_space=pltpu.SMEM), vmem],
        out_specs=[vmem] * (1 + len(SENT)),
        compiler_params=pltpu.CompilerParams(vmem_limit_bytes=VMEM),
        name="pick",
    )(lists, rows)


EARLY = tuple((0, dx) for dx in (0, -1, 1)) + tuple(
    (dz, dx) for dx in (0, -1, 1) for dz in (-1, 1, 2)
)
LATE = tuple((dz, 2) for dz in (0, -1, 1, 2))
ZROWS = SROWS // NZ


def fetch(info, factor, sems, sources):
    zh, x, core = info[0], info[1], info[2]
    copies = {dz: [] for dz in (0, -1, 1, 2)}
    count = 0
    for part, offsets, swapped in sources:
        side = 1 - core if swapped else core
        for p, (dz, dx) in enumerate(offsets):
            base = ((zh + dz + NZ) % NZ * NX + (x + dx + NX) % NX) * 2 + side
            copy = pltpu.make_async_copy(
                part.at[pl.ds(p * ROWS, ROWS), :],
                factor.at[pl.ds(pl.multiple_of(base * ROWS, 32), ROWS), :],
                sems.at[count],
            )
            copy.start()
            copies[dz].append(copy)
            count += 1
    return copies


def stage_kernel(
    info, own_rows, early, early_swapped, sides, sides_swapped,
    factor, wide, token, sems, wide_sem,
):
    wide_copy = pltpu.make_async_copy(own_rows, wide.at[:BS], wide_sem)
    wide_copy.start()
    token[...] = jnp.zeros_like(token)
    sources = (
        (early, EARLY[:6], False),
        (sides, EARLY[6:], False),
        (early_swapped, EARLY[:6], True),
        (sides_swapped, EARLY[6:], True),
    )
    copies = fetch(info, factor, sems, sources)
    for copy in [wide_copy] + sum(copies.values(), []):
        copy.wait()


def stage(info, own_rows, early, early_swapped, sides, sides_swapped):
    smem = pl.BlockSpec(memory_space=pltpu.SMEM)
    vmem = pl.BlockSpec(memory_space=pltpu.VMEM)
    hbm = pl.BlockSpec(memory_space=pl.ANY)
    return pl.pallas_call(
        stage_kernel,
        out_shape=[
            pltpu.VMEM((SROWS, NC), jnp.bfloat16),
            pltpu.VMEM((2 * BS, SROWS), jnp.bfloat16),
            jax.ShapeDtypeStruct((8, BS), jnp.float32),
        ],
        in_specs=[smem, vmem] + [hbm] * 4,
        out_specs=[vmem] * 3,
        scratch_shapes=[
            pltpu.SemaphoreType.DMA((2 * len(EARLY),)),
            pltpu.SemaphoreType.DMA(()),
        ],
        compiler_params=pltpu.CompilerParams(vmem_limit_bytes=VMEM),
        name="stage",
    )(info, own_rows, early, early_swapped, sides, sides_swapped)


def product_kernel(
    info, _, __, ___, rows, late, late_swapped,
    factor, wide, own_out, other_out, turned, total, sems, wide_sem,
):
    wide_copy = pltpu.make_async_copy(rows, wide.at[BS:], wide_sem)
    wide_copy.start()
    sources = ((late, LATE, False), (late_swapped, LATE, True))
    copies = fetch(info, factor, sems, sources)
    wide_copy.wait()
    for s, (dz, waits) in enumerate(copies.items()):
        for copy in waits:
            copy.wait()
        start = pl.multiple_of((info[0] + dz + NZ) % NZ * ZROWS, BS)
        term = jnp.dot(
            wide[:, pl.ds(start, ZROWS)],
            factor[pl.ds(start, ZROWS), :],
            preferred_element_type=jnp.float32,
        )
        if s == 0:
            total[...] = term
        else:
            total[...] += term
    own = jnp.where(info[3] > 0, total[:BS], 0.0)
    other = jnp.where(info[4] > 0, total[BS:], 0.0)
    own_out[...] = -own
    other_out[...] = -other
    turned[:, :BS] = own.T.astype(jnp.bfloat16)
    turned[:, BS:] = other.T.astype(jnp.bfloat16)


def product(info, factor, wide, token, rows, late, late_swapped):
    smem = pl.BlockSpec(memory_space=pltpu.SMEM)
    vmem = pl.BlockSpec(memory_space=pltpu.VMEM)
    hbm = pl.BlockSpec(memory_space=pl.ANY)
    return pl.pallas_call(
        product_kernel,
        out_shape=[
            pltpu.VMEM((SROWS, NC), jnp.bfloat16),
            pltpu.VMEM((2 * BS, SROWS), jnp.bfloat16),
            jax.ShapeDtypeStruct((BS, NC), jnp.float32),
            jax.ShapeDtypeStruct((BS, NC), jnp.float32),
            jax.ShapeDtypeStruct((NC, 2 * BS), jnp.bfloat16),
        ],
        in_specs=[smem, vmem, vmem] + [hbm] * 4,
        out_specs=[vmem] * 5,
        input_output_aliases={1: 0, 2: 1},
        scratch_shapes=[
            pltpu.VMEM((2 * BS, NC), jnp.float32),
            pltpu.SemaphoreType.DMA((2 * len(LATE),)),
            pltpu.SemaphoreType.DMA(()),
        ],
        compiler_params=pltpu.CompilerParams(vmem_limit_bytes=VMEM),
        name="product",
    )(info, factor, wide, token, rows, late, late_swapped)


def partial_kernel(info, turned, factor, out, chosen):
    width = NC // NEAR
    for i in range(2 * NEAR):
        start = pl.multiple_of(info[8 + i] * BS, BS)
        chosen[i * BS : (i + 1) * BS, :] = factor[pl.ds(start, BS), :]
    left = jnp.concatenate(
        [turned[s * width : (s + 1) * width, :] for s in range(NEAR)], axis=1
    )
    total = jnp.dot(left, chosen[...], preferred_element_type=jnp.float32)
    tall = total.T
    for d in range(NBLK):
        first = tall[d * 16 : d * 16 + 8]
        second = tall[d * 16 + 8 : d * 16 + 16]
        out[d * 8 : (d + 1) * 8, :] = jnp.concatenate([first, second], axis=1)


def partial(info, turned, factor):
    smem = pl.BlockSpec(memory_space=pltpu.SMEM)
    vmem = pl.BlockSpec(memory_space=pltpu.VMEM)
    return pl.pallas_call(
        partial_kernel,
        out_shape=jax.ShapeDtypeStruct((NBLK * 8, BS), jnp.float32),
        in_specs=[smem, vmem, vmem],
        out_specs=vmem,
        scratch_shapes=[pltpu.VMEM((2 * NEAR * BS, NC), jnp.bfloat16)],
        compiler_params=pltpu.CompilerParams(vmem_limit_bytes=VMEM),
        name="partial",
    )(info, turned, factor)


def total_kernel(terms, diagonal, out):
    half = BS // 2
    for j in range(NEAR):
        tile = terms[j * 8 : (j + 1) * 8, :]
        for z in range(1, NZ):
            at = (z * NEAR + j) * 8
            tile = tile + terms[at : at + 8, :]
        columns = slice(j * half, (j + 1) * half)
        out[0:8, columns] = diagonal[0:8, columns] + tile[:, :half]
        out[8:16, columns] = diagonal[8:16, columns] + tile[:, half:]


def total(terms, diagonal):
    vmem = pl.BlockSpec(memory_space=pltpu.VMEM)
    return pl.pallas_call(
        total_kernel,
        out_shape=jax.ShapeDtypeStruct((NC // NBLK, NC), jnp.float32),
        in_specs=[vmem, vmem],
        out_specs=vmem,
        name="total",
    )(terms, diagonal)


def other_core(value):
    return ring(value, 0, 0, 1)


def onward(core, right, left):
    return ring(jnp.where(core == 0, right, left), 0, 1, 0, mirrored=True)


def body(parent_inverse, child_factor, child_diagonal, structure):
    blk = lax.axis_index("blk")
    front = lax.axis_index("front")
    half = front % 2
    zh, x, core = blk // NEAR, blk // 2 % NX, blk % 2
    mine = child_factor[0]
    lists = lax.dynamic_slice_in_dim(structure, front - half, 2, 0)
    lists = jnp.where(half == 0, lists, lists[::-1])
    listing = lists[0]
    near_at = zh * NEAR + jnp.arange(NEAR)
    blocks = jnp.stack(
        [half * (NPB // 2) + near_at, (1 - half) * (NPB // 2) + near_at], axis=1
    ).reshape(-1)
    position = jnp.sum((listing[None, :] < blocks[:, None]).astype(jnp.int32), axis=1)
    position = jnp.minimum(position, NS - 1)
    wanted = jnp.stack([half * (NPB // 2) + blk, (1 - half) * (NPB // 2) + blk])
    member = jnp.any(listing[None, :] == wanted[:, None], axis=1).astype(jnp.int32)
    info = jnp.concatenate(
        [jnp.stack([zh, x, core]), member, jnp.zeros((3,), jnp.int32), position]
    )

    near = [mine] + [ring(mine, 0, dx, 0) for dx in (1, -1)]
    up = ring(mine, 1, 0, 0)
    down = ring(mine, -1, 0, 0)
    near, lists, info, up, down = lax.optimization_barrier((near, lists, info, up, down))

    across = ring(jnp.where(core == 0, up, down), 1, 0, 0, mirrored=True)
    own_rows, *sends = pick(lists, parent_inverse[0])
    own_rows, sends, across = lax.optimization_barrier((own_rows, sends, across))
    trio = jnp.concatenate([up, down, across], axis=0)
    right = ring(trio, 0, 1, 0)
    left = ring(trio, 0, -1, 0)
    trio, right, left = lax.optimization_barrier((trio, right, left))
    early = jnp.concatenate([*near, trio], axis=0)
    early_swapped = other_core(early)
    sides = jnp.concatenate([right, left], axis=0)
    sides_swapped = other_core(sides)
    late = onward(
        core,
        jnp.concatenate([near[1], right], axis=0),
        jnp.concatenate([near[2], left], axis=0),
    )
    other_rows = partner(sends[0])
    factor, wide, token = stage(
        info, own_rows, early, early_swapped, sides, sides_swapped
    )
    late, other_rows, token = lax.optimization_barrier((late, other_rows, token))
    late_swapped = other_core(late)
    factor, _, own_out, other_out, turned = product(
        info, factor, wide, token, other_rows, late, late_swapped
    )
    second = partner(other_out)
    groups = [[z * NEAR + i for i in range(NEAR)] for z in range(NZ)]
    turned = lax.all_to_all(
        turned, "blk", 0, 0, axis_index_groups=groups, tiled=True
    )
    terms = lax.all_to_all(partial(info, turned, factor), "blk", 0, 0, tiled=True)
    inverse = total(terms, child_diagonal[0])
    placed = jnp.stack([own_out, second], axis=1)
    return placed[None], inverse[None]


def solution(mesh):
    in_specs = (P("front", "blk", None), P("front", "blk", None), P("front", "blk", None), P())
    out_specs = (P("front", "blk", None, None), P("front", "blk", None))
    return jax.shard_map(body, mesh=mesh, in_specs=in_specs, out_specs=out_specs, check_vma=False)
```

```python
import jax
import jax.numpy as jnp
from jax import lax
from jax.experimental import pallas as pl
from jax.experimental.pallas import tpu as pltpu
from jax.sharding import PartitionSpec as P

BS = 128
NPB = 64
NS = 40
NC = 512
SROWS = NS * BS
NZ = 4
NX = 4
NBLK = NZ * NX * 2
ROWS = SROWS // NBLK
NEAR = NX * 2
VMEM = 32 * 1024 * 1024


def ring(value, dz, dx, swap, mirrored=False):
    pairs = []
    for z in range(NZ):
        for x in range(NX):
            for c in range(2):
                s = -1 if mirrored and c else 1
                to = ((z + s * dz) % NZ * NX + (x + s * dx) % NX) * 2 + (c ^ swap)
                pairs.append(((z * NX + x) * 2 + c, to))
    return lax.ppermute(value, "blk", pairs)


def partner(value):
    pairs = [(source, source ^ 1) for source in range(lax.axis_size("front"))]
    return lax.ppermute(value, "front", pairs)


SENT = (40,)


def pick_kernel(lists, rows, own, *others):
    for i in range(NS):
        columns = pl.ds(pl.multiple_of(lists[0, i] * BS, BS), BS)
        own[:, i * BS : (i + 1) * BS] = rows[:, columns]
    i = 0
    for n, count in enumerate(SENT):
        for at in range(count):
            columns = pl.ds(pl.multiple_of(lists[1, i] * BS, BS), BS)
            others[n][:, at * BS : (at + 1) * BS] = rows[:, columns]
            i += 1


def pick(lists, rows):
    vmem = pl.BlockSpec(memory_space=pltpu.VMEM)
    return pl.pallas_call(
        pick_kernel,
        out_shape=[pltpu.VMEM((BS, SROWS), jnp.bfloat16)]
        + [jax.ShapeDtypeStruct((BS, count * BS), jnp.bfloat16) for count in SENT],
        in_specs=[pl.BlockSpec(memory_space=pltpu.SMEM), vmem],
        out_specs=[vmem] * (1 + len(SENT)),
        compiler_params=pltpu.CompilerParams(vmem_limit_bytes=VMEM),
        name="pick",
    )(lists, rows)


EARLY = tuple((0, dx) for dx in (0, -1, 1)) + tuple(
    (dz, dx) for dx in (0, -1, 1) for dz in (-1, 1, 2)
)
LATE = tuple((dz, 2) for dz in (0, -1, 1, 2))
ZROWS = SROWS // NZ


def fetch(info, factor, sems, sources):
    zh, x, core = info[0], info[1], info[2]
    copies = {dz: [] for dz in (0, -1, 1, 2)}
    count = 0
    for part, offsets, swapped in sources:
        side = 1 - core if swapped else core
        for p, (dz, dx) in enumerate(offsets):
            base = ((zh + dz + NZ) % NZ * NX + (x + dx + NX) % NX) * 2 + side
            copy = pltpu.make_async_copy(
                part.at[pl.ds(p * ROWS, ROWS), :],
                factor.at[pl.ds(pl.multiple_of(base * ROWS, 32), ROWS), :],
                sems.at[count],
            )
            copy.start()
            copies[dz].append(copy)
            count += 1
    return copies


def stage_kernel(
    info, own_rows, early, early_swapped, sides, sides_swapped,
    factor, wide, token, sems, wide_sem,
):
    wide_copy = pltpu.make_async_copy(own_rows, wide.at[:BS], wide_sem)
    wide_copy.start()
    token[...] = jnp.zeros_like(token)
    sources = (
        (early, EARLY[:6], False),
        (sides, EARLY[6:], False),
        (early_swapped, EARLY[:6], True),
        (sides_swapped, EARLY[6:], True),
    )
    copies = fetch(info, factor, sems, sources)
    for copy in [wide_copy] + sum(copies.values(), []):
        copy.wait()


def stage(info, own_rows, early, early_swapped, sides, sides_swapped):
    smem = pl.BlockSpec(memory_space=pltpu.SMEM)
    vmem = pl.BlockSpec(memory_space=pltpu.VMEM)
    hbm = pl.BlockSpec(memory_space=pl.ANY)
    return pl.pallas_call(
        stage_kernel,
        out_shape=[
            pltpu.VMEM((SROWS, NC), jnp.bfloat16),
            pltpu.VMEM((2 * BS, SROWS), jnp.bfloat16),
            jax.ShapeDtypeStruct((8, BS), jnp.float32),
        ],
        in_specs=[smem, vmem] + [hbm] * 4,
        out_specs=[vmem] * 3,
        scratch_shapes=[
            pltpu.SemaphoreType.DMA((2 * len(EARLY),)),
            pltpu.SemaphoreType.DMA(()),
        ],
        compiler_params=pltpu.CompilerParams(vmem_limit_bytes=VMEM),
        name="stage",
    )(info, own_rows, early, early_swapped, sides, sides_swapped)


def product_kernel(
    info, _, __, ___, rows, late, late_swapped,
    factor, wide, own_out, other_out, turned, total, sems, wide_sem,
):
    wide_copy = pltpu.make_async_copy(rows, wide.at[BS:], wide_sem)
    wide_copy.start()
    sources = ((late, LATE, False), (late_swapped, LATE, True))
    copies = fetch(info, factor, sems, sources)
    wide_copy.wait()
    for s, (dz, waits) in enumerate(copies.items()):
        for copy in waits:
            copy.wait()
        start = pl.multiple_of((info[0] + dz + NZ) % NZ * ZROWS, BS)
        term = jnp.dot(
            wide[:, pl.ds(start, ZROWS)],
            factor[pl.ds(start, ZROWS), :],
            preferred_element_type=jnp.float32,
        )
        if s == 0:
            total[...] = term
        else:
            total[...] += term
    own = jnp.where(info[3] > 0, total[:BS], 0.0)
    other = jnp.where(info[4] > 0, total[BS:], 0.0)
    own_out[...] = -own
    other_out[...] = -other
    turned[:, :BS] = own.T.astype(jnp.bfloat16)
    turned[:, BS:] = other.T.astype(jnp.bfloat16)


def product(info, factor, wide, token, rows, late, late_swapped):
    smem = pl.BlockSpec(memory_space=pltpu.SMEM)
    vmem = pl.BlockSpec(memory_space=pltpu.VMEM)
    hbm = pl.BlockSpec(memory_space=pl.ANY)
    return pl.pallas_call(
        product_kernel,
        out_shape=[
            pltpu.VMEM((SROWS, NC), jnp.bfloat16),
            pltpu.VMEM((2 * BS, SROWS), jnp.bfloat16),
            jax.ShapeDtypeStruct((BS, NC), jnp.float32),
            jax.ShapeDtypeStruct((BS, NC), jnp.float32),
            jax.ShapeDtypeStruct((NC, 2 * BS), jnp.bfloat16),
        ],
        in_specs=[smem, vmem, vmem] + [hbm] * 4,
        out_specs=[vmem] * 5,
        input_output_aliases={1: 0, 2: 1},
        scratch_shapes=[
            pltpu.VMEM((2 * BS, NC), jnp.float32),
            pltpu.SemaphoreType.DMA((2 * len(LATE),)),
            pltpu.SemaphoreType.DMA(()),
        ],
        compiler_params=pltpu.CompilerParams(vmem_limit_bytes=VMEM),
        name="product",
    )(info, factor, wide, token, rows, late, late_swapped)


def partial_kernel(info, turned, factor, out, chosen):
    width = NC // NEAR
    for i in range(2 * NEAR):
        start = pl.multiple_of(info[8 + i] * BS, BS)
        chosen[i * BS : (i + 1) * BS, :] = factor[pl.ds(start, BS), :]
    left = jnp.concatenate(
        [turned[s * width : (s + 1) * width, :] for s in range(NEAR)], axis=1
    )
    total = jnp.dot(left, chosen[...], preferred_element_type=jnp.float32)
    tall = total.T
    for d in range(NBLK):
        first = tall[d * 16 : d * 16 + 8]
        second = tall[d * 16 + 8 : d * 16 + 16]
        out[d * 8 : (d + 1) * 8, :] = jnp.concatenate([first, second], axis=1)


def partial(info, turned, factor):
    smem = pl.BlockSpec(memory_space=pltpu.SMEM)
    vmem = pl.BlockSpec(memory_space=pltpu.VMEM)
    return pl.pallas_call(
        partial_kernel,
        out_shape=jax.ShapeDtypeStruct((NBLK * 8, BS), jnp.float32),
        in_specs=[smem, vmem, vmem],
        out_specs=vmem,
        scratch_shapes=[pltpu.VMEM((2 * NEAR * BS, NC), jnp.bfloat16)],
        compiler_params=pltpu.CompilerParams(vmem_limit_bytes=VMEM),
        name="partial",
    )(info, turned, factor)


def total_kernel(terms, diagonal, out, held, base, sems):
    copies = [pltpu.make_async_copy(diagonal, base, sems.at[0])]
    for z in range(NZ):
        rows = pl.ds(z * NEAR * 8, NEAR * 8)
        copies.append(
            pltpu.make_async_copy(terms.at[rows], held.at[rows], sems.at[z + 1])
        )
    for copy in copies:
        copy.start()
    for copy in copies:
        copy.wait()
    half = BS // 2
    for j in range(NEAR):
        tile = held[j * 8 : (j + 1) * 8, :]
        for z in range(1, NZ):
            at = (z * NEAR + j) * 8
            tile = tile + held[at : at + 8, :]
        columns = slice(j * half, (j + 1) * half)
        out[0:8, columns] = base[0:8, columns] + tile[:, :half]
        out[8:16, columns] = base[8:16, columns] + tile[:, half:]


def total(terms, diagonal):
    hbm = pl.BlockSpec(memory_space=pl.ANY)
    return pl.pallas_call(
        total_kernel,
        out_shape=jax.ShapeDtypeStruct((NC // NBLK, NC), jnp.float32),
        in_specs=[hbm, hbm],
        out_specs=pl.BlockSpec(memory_space=pltpu.VMEM),
        scratch_shapes=[
            pltpu.VMEM((NBLK * 8, BS), jnp.float32),
            pltpu.VMEM((NC // NBLK, NC), jnp.float32),
            pltpu.SemaphoreType.DMA((1 + NZ,)),
        ],
        compiler_params=pltpu.CompilerParams(vmem_limit_bytes=60 * 1024 * 1024),
        name="total",
    )(terms, diagonal)


def other_core(value):
    return ring(value, 0, 0, 1)


def onward(core, right, left):
    return ring(jnp.where(core == 0, right, left), 0, 1, 0, mirrored=True)


def body(parent_inverse, child_factor, child_diagonal, structure):
    blk = lax.axis_index("blk")
    front = lax.axis_index("front")
    half = front % 2
    zh, x, core = blk // NEAR, blk // 2 % NX, blk % 2
    mine = child_factor[0]
    lists = lax.dynamic_slice_in_dim(structure, front - half, 2, 0)
    lists = jnp.where(half == 0, lists, lists[::-1])
    listing = lists[0]
    near_at = zh * NEAR + jnp.arange(NEAR)
    blocks = jnp.stack(
        [half * (NPB // 2) + near_at, (1 - half) * (NPB // 2) + near_at], axis=1
    ).reshape(-1)
    position = jnp.sum((listing[None, :] < blocks[:, None]).astype(jnp.int32), axis=1)
    position = jnp.minimum(position, NS - 1)
    wanted = jnp.stack([half * (NPB // 2) + blk, (1 - half) * (NPB // 2) + blk])
    member = jnp.any(listing[None, :] == wanted[:, None], axis=1).astype(jnp.int32)
    info = jnp.concatenate(
        [jnp.stack([zh, x, core]), member, jnp.zeros((3,), jnp.int32), position]
    )

    near = [mine] + [ring(mine, 0, dx, 0) for dx in (1, -1)]
    up = ring(mine, 1, 0, 0)
    down = ring(mine, -1, 0, 0)
    near, lists, info, up, down = lax.optimization_barrier((near, lists, info, up, down))

    across = ring(jnp.where(core == 0, up, down), 1, 0, 0, mirrored=True)
    own_rows, *sends = pick(lists, parent_inverse[0])
    own_rows, sends, across = lax.optimization_barrier((own_rows, sends, across))
    trio = jnp.concatenate([up, down, across], axis=0)
    right = ring(trio, 0, 1, 0)
    left = ring(trio, 0, -1, 0)
    trio, right, left = lax.optimization_barrier((trio, right, left))
    early = jnp.concatenate([*near, trio], axis=0)
    early_swapped = other_core(early)
    sides = jnp.concatenate([right, left], axis=0)
    sides_swapped = other_core(sides)
    late = onward(
        core,
        jnp.concatenate([near[1], right], axis=0),
        jnp.concatenate([near[2], left], axis=0),
    )
    other_rows = partner(sends[0])
    factor, wide, token = stage(
        info, own_rows, early, early_swapped, sides, sides_swapped
    )
    late, other_rows, token = lax.optimization_barrier((late, other_rows, token))
    late_swapped = other_core(late)
    factor, _, own_out, other_out, turned = product(
        info, factor, wide, token, other_rows, late, late_swapped
    )
    second = partner(other_out)
    groups = [[z * NEAR + i for i in range(NEAR)] for z in range(NZ)]
    turned = lax.all_to_all(
        turned, "blk", 0, 0, axis_index_groups=groups, tiled=True
    )
    terms = lax.all_to_all(partial(info, turned, factor), "blk", 0, 0, tiled=True)
    inverse = total(terms, child_diagonal[0])
    placed = jnp.stack([own_out, second], axis=1)
    return placed[None], inverse[None]


def solution(mesh):
    in_specs = (P("front", "blk", None), P("front", "blk", None), P("front", "blk", None), P())
    out_specs = (P("front", "blk", None, None), P("front", "blk", None))
    return jax.shard_map(body, mesh=mesh, in_specs=in_specs, out_specs=out_specs, check_vma=False)
```

```python
import jax
import jax.numpy as jnp
from jax import lax
from jax.experimental import pallas as pl
from jax.experimental.pallas import tpu as pltpu
from jax.sharding import PartitionSpec as P

BS = 128
NPB = 64
NS = 40
NC = 512
SROWS = NS * BS
NZ = 4
NX = 4
NBLK = NZ * NX * 2
ROWS = SROWS // NBLK
NEAR = NX * 2
VMEM = 32 * 1024 * 1024


def ring(value, dz, dx, swap, mirrored=False):
    pairs = []
    for z in range(NZ):
        for x in range(NX):
            for c in range(2):
                s = -1 if mirrored and c else 1
                to = ((z + s * dz) % NZ * NX + (x + s * dx) % NX) * 2 + (c ^ swap)
                pairs.append(((z * NX + x) * 2 + c, to))
    return lax.ppermute(value, "blk", pairs)


def partner(value):
    pairs = [(source, source ^ 1) for source in range(lax.axis_size("front"))]
    return lax.ppermute(value, "front", pairs)


SENT = (40,)


def pick_kernel(lists, rows, own, *others):
    for i in range(NS):
        columns = pl.ds(pl.multiple_of(lists[0, i] * BS, BS), BS)
        own[:, i * BS : (i + 1) * BS] = rows[:, columns]
    i = 0
    for n, count in enumerate(SENT):
        for at in range(count):
            columns = pl.ds(pl.multiple_of(lists[1, i] * BS, BS), BS)
            others[n][:, at * BS : (at + 1) * BS] = rows[:, columns]
            i += 1


def pick(lists, rows):
    vmem = pl.BlockSpec(memory_space=pltpu.VMEM)
    return pl.pallas_call(
        pick_kernel,
        out_shape=[pltpu.VMEM((BS, SROWS), jnp.bfloat16)]
        + [jax.ShapeDtypeStruct((BS, count * BS), jnp.bfloat16) for count in SENT],
        in_specs=[pl.BlockSpec(memory_space=pltpu.SMEM), vmem],
        out_specs=[vmem] * (1 + len(SENT)),
        compiler_params=pltpu.CompilerParams(vmem_limit_bytes=VMEM),
        name="pick",
    )(lists, rows)


EARLY = tuple((0, dx) for dx in (0, -1, 1)) + tuple(
    (dz, dx) for dx in (0, -1, 1) for dz in (-1, 1, 2)
)
LATE = tuple((dz, 2) for dz in (0, -1, 1, 2))
ZROWS = SROWS // NZ


def fetch(info, factor, sems, sources):
    zh, x, core = info[0], info[1], info[2]
    copies = {dz: [] for dz in (0, -1, 1, 2)}
    count = 0
    for part, offsets, swapped in sources:
        side = 1 - core if swapped else core
        for p, (dz, dx) in enumerate(offsets):
            base = ((zh + dz + NZ) % NZ * NX + (x + dx + NX) % NX) * 2 + side
            copy = pltpu.make_async_copy(
                part.at[pl.ds(p * ROWS, ROWS), :],
                factor.at[pl.ds(pl.multiple_of(base * ROWS, 32), ROWS), :],
                sems.at[count],
            )
            copy.start()
            copies[dz].append(copy)
            count += 1
    return copies


def stage_kernel(
    info, own_rows, early, early_swapped, sides, sides_swapped,
    factor, wide, token, sems, wide_sem,
):
    wide_copy = pltpu.make_async_copy(own_rows, wide.at[:BS], wide_sem)
    wide_copy.start()
    token[...] = jnp.zeros_like(token)
    sources = (
        (early, EARLY[:6], False),
        (sides, EARLY[6:], False),
        (early_swapped, EARLY[:6], True),
        (sides_swapped, EARLY[6:], True),
    )
    copies = fetch(info, factor, sems, sources)
    for copy in [wide_copy] + sum(copies.values(), []):
        copy.wait()


def stage(info, own_rows, early, early_swapped, sides, sides_swapped):
    smem = pl.BlockSpec(memory_space=pltpu.SMEM)
    vmem = pl.BlockSpec(memory_space=pltpu.VMEM)
    hbm = pl.BlockSpec(memory_space=pl.ANY)
    return pl.pallas_call(
        stage_kernel,
        out_shape=[
            pltpu.VMEM((SROWS, NC), jnp.bfloat16),
            pltpu.VMEM((2 * BS, SROWS), jnp.bfloat16),
            jax.ShapeDtypeStruct((8, BS), jnp.float32),
        ],
        in_specs=[smem, vmem] + [hbm] * 4,
        out_specs=[vmem] * 3,
        scratch_shapes=[
            pltpu.SemaphoreType.DMA((2 * len(EARLY),)),
            pltpu.SemaphoreType.DMA(()),
        ],
        compiler_params=pltpu.CompilerParams(vmem_limit_bytes=VMEM),
        name="stage",
    )(info, own_rows, early, early_swapped, sides, sides_swapped)


def product_kernel(
    info, _, __, ___, rows, late, late_swapped,
    factor, wide, own_out, other_out, turned, total, sems, wide_sem,
):
    wide_copy = pltpu.make_async_copy(rows, wide.at[BS:], wide_sem)
    wide_copy.start()
    sources = ((late, LATE, False), (late_swapped, LATE, True))
    copies = fetch(info, factor, sems, sources)
    wide_copy.wait()
    for s, (dz, waits) in enumerate(copies.items()):
        for copy in waits:
            copy.wait()
        start = pl.multiple_of((info[0] + dz + NZ) % NZ * ZROWS, BS)
        term = jnp.dot(
            wide[:, pl.ds(start, ZROWS)],
            factor[pl.ds(start, ZROWS), :],
            preferred_element_type=jnp.float32,
        )
        if s == 0:
            total[...] = term
        else:
            total[...] += term
    own = jnp.where(info[3] > 0, total[:BS], 0.0)
    other = jnp.where(info[4] > 0, total[BS:], 0.0)
    own_out[...] = -own
    other_out[...] = -other
    turned[:, :BS] = own.T.astype(jnp.bfloat16)
    turned[:, BS:] = other.T.astype(jnp.bfloat16)


def product(info, factor, wide, token, rows, late, late_swapped):
    smem = pl.BlockSpec(memory_space=pltpu.SMEM)
    vmem = pl.BlockSpec(memory_space=pltpu.VMEM)
    hbm = pl.BlockSpec(memory_space=pl.ANY)
    return pl.pallas_call(
        product_kernel,
        out_shape=[
            pltpu.VMEM((SROWS, NC), jnp.bfloat16),
            pltpu.VMEM((2 * BS, SROWS), jnp.bfloat16),
            jax.ShapeDtypeStruct((BS, NC), jnp.float32),
            jax.ShapeDtypeStruct((BS, NC), jnp.float32),
            jax.ShapeDtypeStruct((NC, 2 * BS), jnp.bfloat16),
        ],
        in_specs=[smem, vmem, vmem] + [hbm] * 4,
        out_specs=[vmem] * 5,
        input_output_aliases={1: 0, 2: 1},
        scratch_shapes=[
            pltpu.VMEM((2 * BS, NC), jnp.float32),
            pltpu.SemaphoreType.DMA((2 * len(LATE),)),
            pltpu.SemaphoreType.DMA(()),
        ],
        compiler_params=pltpu.CompilerParams(vmem_limit_bytes=VMEM),
        name="product",
    )(info, factor, wide, token, rows, late, late_swapped)


def partial_kernel(info, turned, factor, out, chosen):
    width = NC // NEAR
    for i in range(2 * NEAR):
        start = pl.multiple_of(info[8 + i] * BS, BS)
        chosen[i * BS : (i + 1) * BS, :] = factor[pl.ds(start, BS), :]
    left = jnp.concatenate(
        [turned[s * width : (s + 1) * width, :] for s in range(NEAR)], axis=1
    )
    total = jnp.dot(left, chosen[...], preferred_element_type=jnp.float32)
    tall = total.T
    for d in range(NBLK):
        first = tall[d * 16 : d * 16 + 8]
        second = tall[d * 16 + 8 : d * 16 + 16]
        out[d * 8 : (d + 1) * 8, :] = jnp.concatenate([first, second], axis=1)


def partial(info, turned, factor):
    smem = pl.BlockSpec(memory_space=pltpu.SMEM)
    vmem = pl.BlockSpec(memory_space=pltpu.VMEM)
    return pl.pallas_call(
        partial_kernel,
        out_shape=jax.ShapeDtypeStruct((NBLK * 8, BS), jnp.float32),
        in_specs=[smem, vmem, vmem],
        out_specs=vmem,
        scratch_shapes=[pltpu.VMEM((2 * NEAR * BS, NC), jnp.bfloat16)],
        compiler_params=pltpu.CompilerParams(vmem_limit_bytes=VMEM),
        name="partial",
    )(info, turned, factor)


def total_kernel(terms, diagonal, out, held, base, sems):
    copies = [pltpu.make_async_copy(diagonal, base, sems.at[0])]
    for z in range(NZ):
        rows = pl.ds(z * NEAR * 8, NEAR * 8)
        copies.append(
            pltpu.make_async_copy(terms.at[rows], held.at[rows], sems.at[z + 1])
        )
    for copy in copies:
        copy.start()
    for copy in copies:
        copy.wait()
    half = BS // 2
    for j in range(NEAR):
        tile = held[j * 8 : (j + 1) * 8, :]
        for z in range(1, NZ):
            at = (z * NEAR + j) * 8
            tile = tile + held[at : at + 8, :]
        columns = slice(j * half, (j + 1) * half)
        out[0:8, columns] = base[0:8, columns] + tile[:, :half]
        out[8:16, columns] = base[8:16, columns] + tile[:, half:]


def total(terms, diagonal):
    hbm = pl.BlockSpec(memory_space=pltpu.MemorySpace.HBM)
    return pl.pallas_call(
        total_kernel,
        out_shape=jax.ShapeDtypeStruct((NC // NBLK, NC), jnp.float32),
        in_specs=[hbm, hbm],
        out_specs=pl.BlockSpec(memory_space=pltpu.VMEM),
        scratch_shapes=[
            pltpu.VMEM((NBLK * 8, BS), jnp.float32),
            pltpu.VMEM((NC // NBLK, NC), jnp.float32),
            pltpu.SemaphoreType.DMA((1 + NZ,)),
        ],
        compiler_params=pltpu.CompilerParams(vmem_limit_bytes=60 * 1024 * 1024),
        name="total",
    )(terms, diagonal)


def other_core(value):
    return ring(value, 0, 0, 1)


def onward(core, right, left):
    return ring(jnp.where(core == 0, right, left), 0, 1, 0, mirrored=True)


def body(parent_inverse, child_factor, child_diagonal, structure):
    blk = lax.axis_index("blk")
    front = lax.axis_index("front")
    half = front % 2
    zh, x, core = blk // NEAR, blk // 2 % NX, blk % 2
    mine = child_factor[0]
    lists = lax.dynamic_slice_in_dim(structure, front - half, 2, 0)
    lists = jnp.where(half == 0, lists, lists[::-1])
    listing = lists[0]
    near_at = zh * NEAR + jnp.arange(NEAR)
    blocks = jnp.stack(
        [half * (NPB // 2) + near_at, (1 - half) * (NPB // 2) + near_at], axis=1
    ).reshape(-1)
    position = jnp.sum((listing[None, :] < blocks[:, None]).astype(jnp.int32), axis=1)
    position = jnp.minimum(position, NS - 1)
    wanted = jnp.stack([half * (NPB // 2) + blk, (1 - half) * (NPB // 2) + blk])
    member = jnp.any(listing[None, :] == wanted[:, None], axis=1).astype(jnp.int32)
    info = jnp.concatenate(
        [jnp.stack([zh, x, core]), member, jnp.zeros((3,), jnp.int32), position]
    )

    near = [mine] + [ring(mine, 0, dx, 0) for dx in (1, -1)]
    up = ring(mine, 1, 0, 0)
    down = ring(mine, -1, 0, 0)
    near, lists, info, up, down = lax.optimization_barrier((near, lists, info, up, down))

    across = ring(jnp.where(core == 0, up, down), 1, 0, 0, mirrored=True)
    own_rows, *sends = pick(lists, parent_inverse[0])
    own_rows, sends, across = lax.optimization_barrier((own_rows, sends, across))
    trio = jnp.concatenate([up, down, across], axis=0)
    right = ring(trio, 0, 1, 0)
    left = ring(trio, 0, -1, 0)
    trio, right, left = lax.optimization_barrier((trio, right, left))
    early = jnp.concatenate([*near, trio], axis=0)
    early_swapped = other_core(early)
    sides = jnp.concatenate([right, left], axis=0)
    sides_swapped = other_core(sides)
    late = onward(
        core,
        jnp.concatenate([near[1], right], axis=0),
        jnp.concatenate([near[2], left], axis=0),
    )
    other_rows = partner(sends[0])
    factor, wide, token = stage(
        info, own_rows, early, early_swapped, sides, sides_swapped
    )
    late, other_rows, token = lax.optimization_barrier((late, other_rows, token))
    late_swapped = other_core(late)
    factor, _, own_out, other_out, turned = product(
        info, factor, wide, token, other_rows, late, late_swapped
    )
    second = partner(other_out)
    groups = [[z * NEAR + i for i in range(NEAR)] for z in range(NZ)]
    turned = lax.all_to_all(
        turned, "blk", 0, 0, axis_index_groups=groups, tiled=True
    )
    terms = lax.all_to_all(partial(info, turned, factor), "blk", 0, 0, tiled=True)
    inverse = total(terms, child_diagonal[0])
    placed = jnp.stack([own_out, second], axis=1)
    return placed[None], inverse[None]


def solution(mesh):
    in_specs = (P("front", "blk", None), P("front", "blk", None), P("front", "blk", None), P())
    out_specs = (P("front", "blk", None, None), P("front", "blk", None))
    return jax.shard_map(body, mesh=mesh, in_specs=in_specs, out_specs=out_specs, check_vma=False)
```
